32 devices in a mesh: groups: 2 (over x), seq: 16 (over z, y, core).
Axes of the slice: x: 2, y: 2, z: 4, core: 2. Of those that a mesh axis runs over, the one named last changes fastest.
Arguments:
- xbc: bfloat16 [16384, 1408], P(('groups', 'seq')), parts along dimension 0, may hold values from -6 to 6
- dt_raw: float32 [40, 16384], P(None, ('groups', 'seq')), parts along dimension 1, may hold values from -6 to 6
- cotangent: bfloat16 [16384, 1280], P(('groups', 'seq')), parts along dimension 0, may hold values from -0.29882812 to 0.29882812
- conv_weight: float32 [4, 1408], replicated, may hold values from -3 to 3
- conv_bias: float32 [1408], replicated, may hold values from -3 to 3
- dt_bias: float32 [40], replicated, may hold values from -3 to 3
- a_log: float32 [40], replicated, may hold values from -14 to -2.9
- d_skip: float32 [40], replicated, may hold values from 0.25 to 2.5
Outputs:
- grad_xbc: bfloat16 [16384, 1408], P(('groups', 'seq')), parts along dimension 0
- grad_dt_raw: float32 [40, 16384], P(None, ('groups', 'seq')), parts along dimension 1
- grad_conv_weight: float32 [8, 1408], P('groups'), parts along dimension 0
- grad_conv_bias: float32 [2816], P('groups'), parts along dimension 0
- grad_dt_bias: float32 [80], P('groups'), parts along dimension 0
- grad_a_log: float32 [80], P('groups'), parts along dimension 0
- grad_d_skip: float32 [80], P('groups'), parts along dimension 0
The draws below stay inside these ranges and needn't reach their ends.
There are 2 independent parts, one for each index of `groups`. The reference program is written for one: setup_inputs(seed, part) draws one part's arguments, and reference() takes and returns one part's arrays. A program takes and returns all parts, laid end to end along the dimension named above; an argument that names none is the same for every part. Nothing has to cross between parts.
All inputs are finite; a program needn't handle non-finite values.
Results may differ from the reference program's by a relative error of at most 0.011.
Values may be sent and summed in bfloat16 or wider, within the bound.
A program may use at most 192 MiB of HBM per device.

```python
import math
import jax
import jax.numpy as jnp
from jax import lax

HEADS = 40
HEAD_DIM = 32
STATE = 64
KERNEL = 4
BLOCK = 128
INNER = 1280
CONV = 1408
LEN = 8192


def draw_a_log(key, part):
    slow_key, slow_rate_key, fast_key = jax.random.split(jax.random.fold_in(key, 17), 3)
    share = 0.5
    slow = jax.random.uniform(slow_key, (HEADS,), jnp.float32) < share
    slow_rate = jnp.exp(jax.random.uniform(slow_rate_key, (HEADS,), jnp.float32, math.log(0.3), math.log(1.5))) / LEN
    fast_rate = jnp.exp(jax.random.uniform(fast_key, (HEADS,), jnp.float32, math.log(0.015), math.log(0.05)))
    return jnp.log(jnp.where(slow, slow_rate, fast_rate)).astype(jnp.float32)


def steps_of(stream_key, shape, cuts, low, top_value):
    factor_of, own = 1.0, jax.random.fold_in(stream_key, 6)
    for dim, parts in cuts:
        heights = jnp.exp(jax.random.uniform(jax.random.fold_in(own, dim), (parts,), jnp.float32, low / len(cuts), top_value / len(cuts)))
        factor_of = factor_of * jnp.repeat(heights, shape[dim] // parts).reshape([-1 if axis == dim else 1 for axis in range(len(shape))])
    return factor_of


def noise(stream_key, shape, scale, bound, cuts=(), kind=jnp.bfloat16):
    entries = scale * jax.random.normal(stream_key, shape, jnp.float32)
    if cuts:
        entries = entries * steps_of(stream_key, shape, cuts, -0.22, 0.18)
    return jnp.clip(entries, -bound, bound).astype(kind)


def setup_inputs(seed: int = 0, part: int = 0) -> dict:
    streams_of = jax.random.split(jax.random.key(seed), 9)
    part_splits = jax.random.split(jax.random.fold_in(streams_of[8], part), 9)
    return {
        "xbc": noise(part_splits[0], (LEN, CONV), 1.0, 6.0, ((0, 16),)),
        "dt_raw": noise(part_splits[1], (HEADS, LEN), 1.0, 6.0, ((1, 16),), jnp.float32),
        "cotangent": noise(part_splits[2], (LEN, INNER), 0.05, 0.29882812, ((0, 16),)),
        "conv_weight": noise(streams_of[3], (KERNEL, CONV), KERNEL ** -0.5, 3.0, (), jnp.float32),
        "conv_bias": noise(streams_of[4], (CONV,), 0.5, 3.0, (), jnp.float32),
        "dt_bias": noise(streams_of[5], (HEADS,), 0.5, 3.0, (), jnp.float32),
        "a_log": draw_a_log(jax.random.fold_in(streams_of[8], 71), part),
        "d_skip": jnp.clip(jax.random.uniform(streams_of[7], (HEADS,), jnp.float32, 0.25, 2.5), 0.25, 2.5),
    }


def activations(padded, conv_weight, conv_bias):
    row_count = padded.shape[0] - conv_weight.shape[0] + 1
    total = jnp.broadcast_to(conv_bias[None, :], (row_count, conv_bias.shape[0]))
    for offset in range(conv_weight.shape[0]):
        total = total + conv_weight[offset][None, :] * padded[offset:offset + row_count]
    return jax.nn.silu(total).astype(jnp.bfloat16)

@jax.checkpoint
def intra_block(x_part, b_part, c_part, step_size, cumulated):
    row_count = x_part.shape[0]
    heads = step_size.shape[0]
    x_heads = x_part.reshape(row_count, heads, HEAD_DIM)
    inner_scores = jnp.dot(c_part, b_part.T, preferred_element_type=jnp.float32)
    causal = lax.broadcasted_iota(jnp.int32, (row_count, row_count), 0) >= lax.broadcasted_iota(jnp.int32, (row_count, row_count), 1)
    spread = cumulated[:, :, None] - cumulated[:, None, :]
    falloff = jnp.where(causal[None], jnp.exp(jnp.where(causal[None], spread, 0.0)), 0.0)
    weights = (inner_scores[None] * falloff * step_size[:, None, :]).astype(jnp.bfloat16)
    return jnp.einsum('hts,shp->thp', weights, x_heads, preferred_element_type=jnp.float32)

def outputs(x_part, b_part, c_part, step_size, cumulated, state_in, d_skip):
    row_count = x_part.shape[0]
    heads = step_size.shape[0]
    x_heads = x_part.reshape(row_count, heads, HEAD_DIM)
    local_term = intra_block(x_part, b_part, c_part, step_size, cumulated)
    carried_term = jnp.einsum('tn,hnp->thp', c_part.astype(jnp.float32), state_in, precision=lax.Precision.HIGHEST)
    carried_term = carried_term * jnp.exp(cumulated).T[:, :, None]
    skip_term = d_skip[None, :, None] * x_heads.astype(jnp.float32)
    return (local_term + carried_term + skip_term).reshape(row_count, heads * HEAD_DIM)

def local_state(x_part, b_part, step_size, cumulated):
    row_count = x_part.shape[0]
    heads = step_size.shape[0]
    x_heads = x_part.reshape(row_count, heads, HEAD_DIM)
    weights = jnp.exp(cumulated[:, -1:] - cumulated) * step_size
    scaled = x_heads.astype(jnp.float32) * weights.T[:, :, None]
    state_piece = jnp.einsum('tn,thp->hnp', b_part.astype(jnp.float32), scaled, precision=lax.Precision.HIGHEST)
    return (state_piece, jnp.exp(cumulated[:, -1]))

def forward(xbc_wide, dt_raw, conv_weight, conv_bias, dt_bias, a_log, d_skip):
    inner = HEADS * HEAD_DIM
    blocks = LEN // BLOCK
    padded = jnp.concatenate([jnp.zeros((KERNEL - 1, xbc_wide.shape[1]), jnp.float32), xbc_wide], axis=0)
    activ = activations(padded, conv_weight, conv_bias)
    step_size = jax.nn.softplus(dt_raw + dt_bias[:, None])
    rate = -jnp.exp(a_log)[:, None] * step_size
    cumulated = jnp.cumsum(rate.reshape(HEADS, blocks, BLOCK), axis=2).transpose(1, 0, 2)
    step_blocks = step_size.reshape(HEADS, blocks, BLOCK).transpose(1, 0, 2)
    x_blocks = activ[:, :inner].reshape(blocks, BLOCK, inner)
    b_blocks = activ[:, inner:inner + STATE].reshape(blocks, BLOCK, STATE)
    c_blocks = activ[:, inner + STATE:].reshape(blocks, BLOCK, STATE)

    def advance(carried, pieces):
        x_part, b_part, c_part, step_part, cum_part = pieces
        result = outputs(x_part, b_part, c_part, step_part, cum_part, carried, d_skip)
        state_piece, decay = local_state(x_part, b_part, step_part, cum_part)
        return (decay[:, None, None] * carried + state_piece, result)
    start = jnp.zeros((HEADS, STATE, HEAD_DIM), jnp.float32)
    final_state, results = lax.scan(advance, start, (x_blocks, b_blocks, c_blocks, step_blocks, cumulated))
    return results.reshape(LEN, inner)

def reference(xbc, dt_raw, cotangent, conv_weight, conv_bias, dt_bias, a_log, d_skip):
    result, backward = jax.vjp(forward, xbc.astype(jnp.float32), dt_raw, conv_weight, conv_bias, dt_bias, a_log, d_skip)
    grads = backward(cotangent.astype(jnp.float32))
    return (grads[0].astype(jnp.bfloat16), grads[1], grads[2], grads[3], grads[4], grads[5], grads[6])
```

```python
import functools

import jax
import jax.numpy as jnp
from jax import lax
from jax.experimental import pallas as pl
from jax.experimental.pallas import tpu as pltpu
from jax.sharding import PartitionSpec as P

HEADS = 40
HEAD_DIM = 32
STATE = 64
BLOCK = 128
INNER = HEADS * HEAD_DIM
CONV = INNER + 2 * STATE
MEMBERS = 4
SLICE = STATE // MEMBERS
F32 = jnp.float32
BF16 = jnp.bfloat16
EXACT = lax.Precision.HIGHEST


def mm(a, b, ca, cb, precision=None):
    return lax.dot_general(
        a, b, (((ca,), (cb,)), ((), ())), precision=precision, preferred_element_type=F32
    )


def iota(shape, dim):
    return lax.broadcasted_iota(jnp.int32, shape, dim)


def split(v):
    high = v.astype(BF16)
    return high, (v - high.astype(F32)).astype(BF16)


def column(row):
    width = row.shape[1]
    eye = iota((width, width), 0) == iota((width, width), 1)
    return jnp.sum(jnp.where(eye, jnp.broadcast_to(row, (width, width)), 0.0), axis=1, keepdims=True)


def kernel(
    n,
    x_ref, dt_ref, cot_ref, w_ref, bias_ref, dtb_ref, alog_ref, skip_ref,
    gx_ref, gdt_ref, gw_ref, gbias_ref, gdtb_ref, galog_ref, gskip_ref,
    xs, edge, act, dsil, xt, gt, fx, u_ref, v_ref, ds_ref, piece, back, fall_ref,
    step_ref, sig_ref, msg, r1, msg2, r2, msg3, r3, cin, ain, dz, dz_edge, prm, p1, p2s, p2,
    edge_sem, s1, q1, s2, q2, s3, q3, dz_sem, s4, q4, s5, q5,
):
    rows = x_ref.shape[0]
    blocks = rows // BLOCK
    groups = n // MEMBERS
    me = lax.axis_index("seq")
    g = me // MEMBERS
    m = me % MEMBERS
    base = g * MEMBERS

    def remote(src, dst, send, recv, to):
        return pltpu.make_async_remote_copy(
            src_ref=src, dst_ref=dst, send_sem=send, recv_sem=recv,
            device_id={"seq": to}, device_id_type=pl.DeviceIdType.MESH,
        )

    barrier = pltpu.get_barrier_semaphore()

    def greet(k, carry):
        pl.semaphore_signal(
            barrier, inc=1, device_id={"seq": (me + k) % n}, device_id_type=pl.DeviceIdType.MESH
        )
        return carry

    lax.fori_loop(1, n, greet, 0)
    pl.semaphore_wait(barrier, n - 1)

    def edge_copy():
        return remote(
            x_ref.at[pl.ds(rows - 16, 16)], edge, edge_sem.at[0], edge_sem.at[1],
            jnp.minimum(me + 1, n - 1),
        )

    @pl.when(me < n - 1)
    def _():
        edge_copy().start()

    alog = column(alog_ref[...])
    neg_a = -jnp.exp(alog)
    raw = dt_ref[...] + column(dtb_ref[...])
    step = jnp.maximum(raw, 0.0) + jnp.log1p(jnp.exp(-jnp.abs(raw)))
    step_ref[...] = step
    sig_ref[...] = 1.0 / (1.0 + jnp.exp(-raw))
    later = iota((BLOCK, BLOCK), 0) <= iota((BLOCK, BLOCK), 1)
    tri = jnp.where(later, 1.0, 0.0)
    causal = iota((BLOCK, BLOCK), 0) >= iota((BLOCK, BLOCK), 1)
    head_row = iota((2 * HEADS, INNER), 0)
    head_row = jnp.where(head_row >= HEADS, head_row - HEADS, head_row)
    spread2 = jnp.where((iota((2 * HEADS, INNER), 1) >> 5) == head_row, 1.0, 0.0).astype(BF16)
    spread_f = jnp.where((iota((HEADS, INNER), 1) >> 5) == iota((HEADS, INNER), 0), 1.0, 0.0)
    spread1 = spread_f.astype(BF16)

    def expand(v):
        high = v.astype(BF16).astype(F32)
        both = jnp.concatenate([high, v - high], axis=0).astype(BF16)
        return mm(both, spread2, 0, 0)

    def per_head(v):
        high, low = split(v)
        return mm(spread1, high, 1, 1) + mm(spread1, low, 1, 1)

    xs[pl.ds(8, rows)] = x_ref[...].astype(F32)
    for b in list(range(1, blocks)) + [0]:
        t0 = b * BLOCK
        if b == 0:
            xs[pl.ds(0, 8)] = jnp.zeros((8, CONV), F32)

            @pl.when(me > 0)
            def _():
                edge_copy().wait_recv()
                xs[pl.ds(0, 8)] = edge[...].astype(F32)[8:16]

        for j in range(CONV // 128):
            lanes = pl.ds(j * 128, 128)
            z = jnp.broadcast_to(bias_ref[:, lanes], (BLOCK, 128))
            for k in range(4):
                z = z + w_ref[pl.ds(k, 1), lanes] * xs[pl.ds(t0 + 5 + k, BLOCK), lanes]
            s = 1.0 / (1.0 + jnp.exp(-z))
            act[pl.ds(t0, BLOCK), lanes] = (z * s).astype(BF16)
            dsil[pl.ds(t0, BLOCK), lanes] = s * (1.0 + z * (1.0 - s))

        rate = neg_a * step_ref[:, pl.ds(t0, BLOCK)]
        cum = mm(rate, tri, 1, 0, EXACT)
        grow = expand(jnp.exp(cum))
        fade = expand(jnp.exp(-cum) * step_ref[:, pl.ds(t0, BLOCK)])
        fx[pl.ds(t0, BLOCK)] = fade
        fall_ref[pl.ds(b * 8, 8)] = jnp.broadcast_to(grow[BLOCK - 1 : BLOCK], (8, INNER))
        xtb = (fade * act[pl.ds(t0, BLOCK), pl.ds(0, INNER)].astype(F32)).astype(BF16)
        gtb = (grow * cot_ref[pl.ds(t0, BLOCK)].astype(F32)).astype(BF16)
        xt[pl.ds(t0, BLOCK)] = xtb
        gt[pl.ds(t0, BLOCK)] = gtb
        bc = act[pl.ds(t0, BLOCK), pl.ds(INNER, 2 * STATE)]
        piece[pl.ds(b * STATE, STATE)] = mm(bc, xtb, 0, 0)[:STATE]
        back[pl.ds(b * STATE, STATE)] = mm(bc, gtb, 0, 0)[STATE:]

    state = jnp.zeros((STATE, INNER), F32)
    adj = jnp.zeros((STATE, INNER), F32)
    decay = jnp.ones((1, INNER), F32)
    for b in range(blocks):
        fall = fall_ref[pl.ds(b * 8, 1)]
        state = fall * (state + piece[pl.ds(b * STATE, STATE)])
        decay = decay * fall
    for b in reversed(range(blocks)):
        adj = fall_ref[pl.ds(b * 8, 1)] * adj + back[pl.ds(b * STATE, STATE)]

    def pack_decay(d):
        d16 = jnp.broadcast_to(d, (SLICE, INNER))
        high = d16.astype(BF16).astype(F32)
        rest = d16 - high
        mid = rest.astype(BF16).astype(F32)
        low = rest - mid
        at = iota((SLICE, INNER), 0)
        return jnp.where(at == 0, high, jnp.where(at == 1, mid, jnp.where(at == 2, low, 0.0))).astype(BF16)

    def unpack_decay(d):
        return jnp.sum(d.astype(F32), axis=0, keepdims=True)

    packed = pack_decay(decay)
    for j in range(MEMBERS):
        msg[j, pl.ds(0, SLICE)] = state[j * SLICE : (j + 1) * SLICE].astype(BF16)
        msg[j, pl.ds(SLICE, SLICE)] = packed
        msg[j, pl.ds(2 * SLICE, SLICE)] = adj[j * SLICE : (j + 1) * SLICE].astype(BF16)

    def round1(off):
        to = (m + off) % MEMBERS
        return remote(msg.at[to], r1.at[m], s1.at[off], q1.at[off], base + to)

    def round1_in(off):
        frm = (m + MEMBERS - off) % MEMBERS
        return remote(msg.at[frm], r1.at[frm], s1.at[off], q1.at[off], base + frm)

    for off in range(1, MEMBERS):
        round1(off).start()
    r1[m] = msg[m]

    def intra(b):
        t0 = b * BLOCK
        bc = act[pl.ds(t0, BLOCK), pl.ds(INNER, 2 * STATE)]
        xtb, gtb = xt[pl.ds(t0, BLOCK)], gt[pl.ds(t0, BLOCK)]
        scores = mm(bc[:, STATE:], bc[:, :STATE], 1, 1)
        smb = jnp.where(causal, scores, 0.0).astype(BF16)
        u_ref[pl.ds(t0, BLOCK)] = mm(smb, xtb, 1, 0)
        v_ref[pl.ds(t0, BLOCK)] = mm(smb, gtb, 0, 0)
        ds_ref[pl.ds(t0, BLOCK)] = jnp.where(causal, mm(gtb, xtb, 1, 1), 0.0).astype(BF16)

    half = blocks // 2
    for b in range(half):
        intra(b)

    for off in range(1, MEMBERS):
        round1_in(off).wait_recv()
    decays = [unpack_decay(r1[i, pl.ds(SLICE, SLICE)]) for i in range(MEMBERS)]
    gs = jnp.zeros((SLICE, INNER), F32)
    ga = jnp.zeros((SLICE, INNER), F32)
    gd = jnp.ones((1, INNER), F32)
    for i in range(MEMBERS):
        gs = decays[i] * gs + r1[i, pl.ds(0, SLICE)].astype(F32)
        gd = gd * decays[i]
    for i in reversed(range(MEMBERS)):
        ga = decays[i] * ga + r1[i, pl.ds(2 * SLICE, SLICE)].astype(F32)
    msg2[pl.ds(0, SLICE)] = gs.astype(BF16)
    msg2[pl.ds(SLICE, SLICE)] = pack_decay(gd)
    msg2[pl.ds(2 * SLICE, SLICE)] = ga.astype(BF16)

    def round2(off):
        to = (g + off) % groups
        part = pl.ds(pl.multiple_of(jnp.where(to > g, 0, SLICE), SLICE), 2 * SLICE)
        return remote(
            msg2.at[part], r2.at[g, part], s2.at[off], q2.at[off], to * MEMBERS + m
        )

    def round2_in(off):
        frm = (g + groups - off) % groups
        part = pl.ds(pl.multiple_of(jnp.where(g > frm, 0, SLICE), SLICE), 2 * SLICE)
        return remote(
            msg2.at[part], r2.at[frm, part], s2.at[off], q2.at[off], frm * MEMBERS + m
        )

    for off in range(1, groups):
        round2(off).start()
    for b in range(half, blocks):
        intra(b)
    cin[...] = jnp.zeros((SLICE, INNER), F32)
    ain[...] = jnp.zeros((SLICE, INNER), F32)
    for off in range(1, groups):
        round2_in(off).wait_recv()
    for q in range(groups):
        @pl.when(q < g)
        def _(q=q):
            d = unpack_decay(r2[q, pl.ds(SLICE, SLICE)])
            cin[...] = d * cin[...] + r2[q, pl.ds(0, SLICE)].astype(F32)
    for q in reversed(range(groups)):
        @pl.when(q > g)
        def _(q=q):
            d = unpack_decay(r2[q, pl.ds(SLICE, SLICE)])
            ain[...] = d * ain[...] + r2[q, pl.ds(2 * SLICE, SLICE)].astype(F32)
    gs = cin[...]
    for i in range(MEMBERS):
        msg3[i, pl.ds(0, SLICE)] = gs.astype(BF16)
        gs = decays[i] * gs + r1[i, pl.ds(0, SLICE)].astype(F32)
    ga = ain[...]
    for i in reversed(range(MEMBERS)):
        msg3[i, pl.ds(SLICE, SLICE)] = ga.astype(BF16)
        ga = decays[i] * ga + r1[i, pl.ds(2 * SLICE, SLICE)].astype(F32)

    def round3(off):
        to = (m + off) % MEMBERS
        return remote(msg3.at[to], r3.at[m], s3.at[off], q3.at[off], base + to)

    def round3_in(off):
        frm = (m + MEMBERS - off) % MEMBERS
        return remote(msg3.at[frm], r3.at[frm], s3.at[off], q3.at[off], base + frm)

    for off in range(1, MEMBERS):
        round3(off).start()
    r3[m] = msg3[m]
    skip = mm(jnp.broadcast_to(skip_ref[...], (8, HEADS)), spread_f, 1, 0, EXACT)[:1]
    skip_sum = jnp.zeros((1, INNER), F32)
    for b in range(blocks):
        rows_b = pl.ds(b * BLOCK, BLOCK)
        skip_sum = skip_sum + jnp.sum(
            cot_ref[rows_b].astype(F32) * act[rows_b, pl.ds(0, INNER)].astype(F32),
            axis=0, keepdims=True,
        )
    prm[...] = jnp.zeros((8, CONV), F32)
    prm[pl.ds(7, 1), pl.ds(0, HEADS)] = mm(
        jnp.broadcast_to(skip_sum, (8, INNER)), spread_f, 1, 1, EXACT
    )[:1]
    for off in range(1, MEMBERS):
        round3_in(off).wait_recv()

    state = jnp.concatenate([r3[i, pl.ds(0, SLICE)].astype(F32) for i in range(MEMBERS)], axis=0)
    adj = jnp.concatenate([r3[i, pl.ds(SLICE, SLICE)].astype(F32) for i in range(MEMBERS)], axis=0)
    for b in range(blocks):
        part = pl.ds(b * STATE, STATE)
        fresh = fall_ref[pl.ds(b * 8, 1)] * (state + piece[part])
        piece[part] = state
        state = fresh
    tails = [None] * blocks
    for b in reversed(range(blocks)):
        part = pl.ds(b * STATE, STATE)
        after = state if b == blocks - 1 else piece[pl.ds((b + 1) * STATE, STATE)]
        tails[b] = jnp.sum(adj * after, axis=0, keepdims=True)
        lent = fall_ref[pl.ds(b * 8, 1)] * adj
        adj = lent + back[part]
        back[part] = lent

    def dz_copy():
        return remote(
            dz.at[pl.ds(0, 8)], dz_edge, dz_sem.at[0], dz_sem.at[1], jnp.maximum(me - 1, 0)
        )

    alog_sum = jnp.zeros((HEADS, BLOCK), F32)
    dtb_sum = jnp.zeros((HEADS, BLOCK), F32)
    last_row = iota((BLOCK, 1), 0) == BLOCK - 1
    for b in range(blocks):
        t0 = b * BLOCK
        here = pl.ds(t0, BLOCK)
        part = pl.ds(b * STATE, STATE)
        xtb, gtb = xt[here], gt[here]
        bc = act[here, pl.ds(INNER, 2 * STATE)]
        bm, cm = bc[:, :STATE], bc[:, STATE:]
        carry_b = piece[part].astype(BF16)
        lent_b = back[part].astype(BF16)
        u = u_ref[here] + mm(cm, carry_b, 1, 0)
        v = v_ref[here] + mm(bm, lent_b, 1, 0)
        taken = xtb.astype(F32) * v
        moved = gtb.astype(F32) * u - taken + jnp.where(last_row, tails[b], 0.0)
        gcum = per_head(moved)
        step_b = step_ref[:, here]
        grate = mm(gcum, tri, 1, 1, EXACT)
        gstep = per_head(taken) / step_b + neg_a * grate
        alog_sum = alog_sum + grate * (neg_a * step_b)
        graw = gstep * sig_ref[:, here]
        gdt_ref[:, here] = graw
        dtb_sum = dtb_sum + graw
        gact = fx[here] * v + skip * cot_ref[here].astype(F32)
        dz[here, pl.ds(0, INNER)] = gact * dsil[here, pl.ds(0, INNER)]
        ds = ds_ref[here]
        gb = mm(ds, cm, 0, 0) + mm(xtb, lent_b, 1, 1)
        gc = mm(ds, bm, 1, 0) + mm(gtb, carry_b, 1, 1)
        dz[here, pl.ds(INNER, 2 * STATE)] = (
            jnp.concatenate([gb, gc], axis=1) * dsil[here, pl.ds(INNER, 2 * STATE)]
        )
        if b == 0:
            @pl.when(me > 0)
            def _():
                dz_copy().start()

    ones = jnp.ones((8, BLOCK), F32)
    prm[pl.ds(5, 1), pl.ds(0, HEADS)] = mm(ones, dtb_sum, 1, 1, EXACT)[:1]
    prm[pl.ds(6, 1), pl.ds(0, HEADS)] = mm(ones, alog_sum, 1, 1, EXACT)[:1]
    for j in range(CONV // 128):
        lanes = pl.ds(j * 128, 128)
        total = [jnp.zeros((8, 128), F32) for _ in range(5)]
        for b in range(blocks):
            t0 = b * BLOCK
            grad = dz[pl.ds(t0, BLOCK), lanes]
            for k in range(4):
                total[k] = total[k] + jnp.sum(
                    (grad * xs[pl.ds(t0 + 5 + k, BLOCK), lanes]).reshape(BLOCK // 8, 8, 128), axis=0
                )
            total[4] = total[4] + jnp.sum(grad.reshape(BLOCK // 8, 8, 128), axis=0)
        for k in range(5):
            prm[pl.ds(k, 1), lanes] = jnp.sum(total[k], axis=0, keepdims=True)

    def sum1(off):
        to = (m + off) % MEMBERS
        return remote(prm, p1.at[m], s4.at[off], q4.at[off], base + to)

    def sum1_in(off):
        frm = (m + MEMBERS - off) % MEMBERS
        return remote(prm, p1.at[frm], s4.at[off], q4.at[off], base + frm)

    def sum2(off):
        to = (g + off) % groups
        return remote(p2s, p2.at[g], s5.at[off], q5.at[off], to * MEMBERS + m)

    def sum2_in(off):
        frm = (g + groups - off) % groups
        return remote(p2s, p2.at[frm], s5.at[off], q5.at[off], frm * MEMBERS + m)

    for off in range(1, MEMBERS):
        sum1(off).start()
    p1[m] = prm[...]

    def data_grad(b):
        t0 = b * BLOCK
        for j in range(CONV // 128):
            lanes = pl.ds(j * 128, 128)
            total = w_ref[pl.ds(0, 1), lanes] * dz[pl.ds(t0 + 3, BLOCK), lanes]
            for k in range(1, 4):
                total = total + w_ref[pl.ds(k, 1), lanes] * dz[pl.ds(t0 + 3 - k, BLOCK), lanes]
            gx_ref[pl.ds(t0, BLOCK), lanes] = total.astype(BF16)

    for b in range(half):
        data_grad(b)
    for off in range(1, MEMBERS):
        sum1_in(off).wait_recv()
    p2s[...] = (p1[0] + p1[1]) + (p1[2] + p1[3])
    for off in range(1, groups):
        sum2(off).start()
    p2[g] = p2s[...]
    dz[pl.ds(rows, 8)] = jnp.zeros((8, CONV), F32)

    @pl.when(me < n - 1)
    def _():
        dz_copy().wait_recv()
        dz[pl.ds(rows, 8)] = dz_edge[...]

    for b in range(half, blocks):
        data_grad(b)
    for off in range(1, groups):
        sum2_in(off).wait_recv()
    total = p2[0]
    for q in range(1, groups):
        total = total + p2[q]
    gw_ref[...] = total[:4]
    gbias_ref[...] = total[4:5]
    gdtb_ref[...] = total[5:6, :HEADS]
    galog_ref[...] = total[6:7, :HEADS]
    gskip_ref[...] = total[7:8, :HEADS]

    @pl.when(me < n - 1)
    def _():
        edge_copy().wait_send()

    @pl.when(me > 0)
    def _():
        dz_copy().wait_send()

    for off in range(1, MEMBERS):
        round1(off).wait_send()
        round3(off).wait_send()
        sum1(off).wait_send()
    for off in range(1, groups):
        round2(off).wait_send()
        sum2(off).wait_send()


def local(n, xbc, dt_raw, cotangent, conv_weight, conv_bias, dt_bias, a_log, d_skip):
    rows = xbc.shape[0]
    blocks = rows // BLOCK
    groups = n // MEMBERS
    vmem = pl.BlockSpec(memory_space=pltpu.VMEM)
    dma = pltpu.SemaphoreType.DMA
    outs = pl.pallas_call(
        functools.partial(kernel, n),
        out_shape=(
            jax.ShapeDtypeStruct((rows, CONV), BF16),
            jax.ShapeDtypeStruct((HEADS, rows), F32),
            jax.ShapeDtypeStruct((4, CONV), F32),
            jax.ShapeDtypeStruct((1, CONV), F32),
            jax.ShapeDtypeStruct((1, HEADS), F32),
            jax.ShapeDtypeStruct((1, HEADS), F32),
            jax.ShapeDtypeStruct((1, HEADS), F32),
        ),
        in_specs=[vmem] * 8,
        out_specs=(vmem,) * 7,
        scratch_shapes=[
            pltpu.VMEM((rows + 8, CONV), F32),
            pltpu.VMEM((16, CONV), BF16),
            pltpu.VMEM((rows, CONV), BF16),
            pltpu.VMEM((rows, CONV), F32),
            pltpu.VMEM((rows, INNER), BF16),
            pltpu.VMEM((rows, INNER), BF16),
            pltpu.VMEM((rows, INNER), F32),
            pltpu.VMEM((rows, INNER), F32),
            pltpu.VMEM((rows, INNER), F32),
            pltpu.VMEM((rows, BLOCK), BF16),
            pltpu.VMEM((blocks * STATE, INNER), F32),
            pltpu.VMEM((blocks * STATE, INNER), F32),
            pltpu.VMEM((blocks * 8, INNER), F32),
            pltpu.VMEM((HEADS, rows), F32),
            pltpu.VMEM((HEADS, rows), F32),
            pltpu.VMEM((MEMBERS, 3 * SLICE, INNER), BF16),
            pltpu.VMEM((MEMBERS, 3 * SLICE, INNER), BF16),
            pltpu.VMEM((3 * SLICE, INNER), BF16),
            pltpu.VMEM((groups, 3 * SLICE, INNER), BF16),
            pltpu.VMEM((MEMBERS, 2 * SLICE, INNER), BF16),
            pltpu.VMEM((MEMBERS, 2 * SLICE, INNER), BF16),
            pltpu.VMEM((SLICE, INNER), F32),
            pltpu.VMEM((SLICE, INNER), F32),
            pltpu.VMEM((rows + 8, CONV), F32),
            pltpu.VMEM((8, CONV), F32),
            pltpu.VMEM((8, CONV), F32),
            pltpu.VMEM((MEMBERS, 8, CONV), F32),
            pltpu.VMEM((8, CONV), F32),
            pltpu.VMEM((groups, 8, CONV), F32),
            dma((2,)),
            dma((MEMBERS,)), dma((MEMBERS,)),
            dma((groups,)), dma((groups,)),
            dma((MEMBERS,)), dma((MEMBERS,)),
            dma((2,)),
            dma((MEMBERS,)), dma((MEMBERS,)),
            dma((groups,)), dma((groups,)),
        ],
        compiler_params=pltpu.CompilerParams(
            collective_id=0, has_side_effects=True, vmem_limit_bytes=56 * 1024 * 1024
        ),
        cost_estimate=pl.CostEstimate(
            flops=2 * 10**9, bytes_accessed=5 * 10**6, transcendentals=10**6
        ),
        name="mixer",
    )(
        xbc, dt_raw, cotangent, conv_weight, conv_bias.reshape(1, CONV),
        dt_bias.reshape(1, HEADS), a_log.reshape(1, HEADS), d_skip.reshape(1, HEADS),
    )
    return (
        outs[0], outs[1], outs[2], outs[3].reshape(CONV), outs[4].reshape(HEADS),
        outs[5].reshape(HEADS), outs[6].reshape(HEADS),
    )


def solution(mesh):
    sequence = P(("groups", "seq"), None)
    return jax.shard_map(
        functools.partial(local, mesh.shape["seq"]),
        mesh=mesh,
        in_specs=(sequence, P(None, ("groups", "seq")), sequence, P(), P(), P(), P(), P()),
        out_specs=(
            sequence, P(None, ("groups", "seq")), P("groups", None),
            P("groups"), P("groups"), P("groups"), P("groups"),
        ),
        check_vma=False,
    )
```

```python
import functools

import jax
import jax.numpy as jnp
from jax import lax
from jax.experimental import pallas as pl
from jax.experimental.pallas import tpu as pltpu
from jax.sharding import PartitionSpec as P

HEADS = 40
HEAD_DIM = 32
STATE = 64
BLOCK = 128
INNER = HEADS * HEAD_DIM
CONV = INNER + 2 * STATE
MEMBERS = 4
SLICE = STATE // MEMBERS
CUTS = 2
WIDTH = INNER // CUTS
F32 = jnp.float32
BF16 = jnp.bfloat16
EXACT = lax.Precision.HIGHEST


def mm(a, b, ca, cb, precision=None):
    return lax.dot_general(
        a, b, (((ca,), (cb,)), ((), ())), precision=precision, preferred_element_type=F32
    )


def iota(shape, dim):
    return lax.broadcasted_iota(jnp.int32, shape, dim)


def split(v):
    high = v.astype(BF16)
    return high, (v - high.astype(F32)).astype(BF16)


def column(row):
    width = row.shape[1]
    eye = iota((width, width), 0) == iota((width, width), 1)
    return jnp.sum(jnp.where(eye, jnp.broadcast_to(row, (width, width)), 0.0), axis=1, keepdims=True)


def kernel(
    n,
    x_ref, dt_ref, cot_ref, w_ref, bias_ref, dtb_ref, alog_ref, skip_ref,
    gx_ref, gdt_ref, sums_ref,
    xs, edge, act, dsil, xt, gt, fx, u_ref, v_ref, ds_ref, piece, back, fall_ref,
    step_ref, sig_ref, msg, r1, msg2, r2, msg3, r3, cin, ain, dz, dz_edge, prm, p1, p2s, p2,
    dec, dall, dexp,
    edge_sem, s1, q1, s2, q2, s3, q3, dz_sem, s4, q4, s5, q5, s6, q6,
):
    rows = x_ref.shape[0]
    blocks = rows // BLOCK
    groups = n // MEMBERS
    me = lax.axis_index("seq")
    g = me // MEMBERS
    m = me % MEMBERS
    base = g * MEMBERS

    def remote(src, dst, send, recv, to):
        return pltpu.make_async_remote_copy(
            src_ref=src, dst_ref=dst, send_sem=send, recv_sem=recv,
            device_id={"seq": to}, device_id_type=pl.DeviceIdType.MESH,
        )

    barrier = pltpu.get_barrier_semaphore()

    def greet(k, carry):
        pl.semaphore_signal(
            barrier, inc=1, device_id={"seq": (me + k) % n}, device_id_type=pl.DeviceIdType.MESH
        )
        return carry

    lax.fori_loop(1, n, greet, 0)
    pl.semaphore_wait(barrier, n - 1)

    def edge_copy():
        return remote(
            x_ref.at[pl.ds(rows - 16, 16)], edge, edge_sem.at[0], edge_sem.at[1],
            jnp.minimum(me + 1, n - 1),
        )

    @pl.when(me < n - 1)
    def _():
        edge_copy().start()

    alog = column(alog_ref[...])
    neg_a = -jnp.exp(alog)
    raw = dt_ref[...] + column(dtb_ref[...])
    step = jnp.maximum(raw, 0.0) + jnp.log1p(jnp.exp(-jnp.abs(raw)))
    step_ref[...] = step
    sig_ref[...] = 1.0 / (1.0 + jnp.exp(-raw))
    later = iota((BLOCK, BLOCK), 0) <= iota((BLOCK, BLOCK), 1)
    tri = jnp.where(later, 1.0, 0.0)
    causal = iota((BLOCK, BLOCK), 0) >= iota((BLOCK, BLOCK), 1)
    head_row = iota((2 * HEADS, INNER), 0)
    head_row = jnp.where(head_row >= HEADS, head_row - HEADS, head_row)
    spread2 = jnp.where((iota((2 * HEADS, INNER), 1) >> 5) == head_row, 1.0, 0.0).astype(BF16)
    spread_f = jnp.where((iota((HEADS, INNER), 1) >> 5) == iota((HEADS, INNER), 0), 1.0, 0.0)
    spread1 = spread_f.astype(BF16)

    def expand(v):
        high = v.astype(BF16).astype(F32)
        both = jnp.concatenate([high, v - high], axis=0).astype(BF16)
        return mm(both, spread2, 0, 0)

    def per_head(v):
        high, low = split(v)
        return mm(spread1, high, 1, 1) + mm(spread1, low, 1, 1)

    total_rate = mm(jnp.ones((8, rows), F32), neg_a * step, 1, 1, EXACT)
    dec[...] = jnp.zeros((8, 128), F32)
    dec[:, pl.ds(0, HEADS)] = jnp.exp(total_rate)

    def decay_out(off):
        return remote(dec, dall.at[me], s6.at[off], q6.at[off], (me + off) % n)

    def decay_in(off):
        frm = (me + n - off) % n
        return remote(dec, dall.at[frm], s6.at[off], q6.at[off], frm)

    def decay_start(off, carry):
        decay_out(off).start()
        return carry

    def decay_wait(off, carry):
        decay_in(off).wait_recv()
        return carry

    def decay_sent(off, carry):
        decay_out(off).wait_send()
        return carry

    lax.fori_loop(1, n, decay_start, 0)
    dall[me] = dec[...]

    xs[pl.ds(8, rows)] = x_ref[...].astype(F32)
    for b in list(range(1, blocks)) + [0]:
        t0 = b * BLOCK
        if b == 0:
            xs[pl.ds(0, 8)] = jnp.zeros((8, CONV), F32)

            @pl.when(me > 0)
            def _():
                edge_copy().wait_recv()
                xs[pl.ds(0, 8)] = edge[...].astype(F32)[8:16]

        for j in range(CONV // 128):
            lanes = pl.ds(j * 128, 128)
            z = jnp.broadcast_to(bias_ref[lanes].reshape(1, 128), (BLOCK, 128))
            for k in range(4):
                z = z + w_ref[pl.ds(k, 1), lanes] * xs[pl.ds(t0 + 5 + k, BLOCK), lanes]
            s = 1.0 / (1.0 + jnp.exp(-z))
            act[pl.ds(t0, BLOCK), lanes] = (z * s).astype(BF16)
            dsil[pl.ds(t0, BLOCK), lanes] = s * (1.0 + z * (1.0 - s))

        rate = neg_a * step_ref[:, pl.ds(t0, BLOCK)]
        cum = mm(rate, tri, 1, 0, EXACT)
        grow = expand(jnp.exp(cum))
        fade = expand(jnp.exp(-cum) * step_ref[:, pl.ds(t0, BLOCK)])
        fx[pl.ds(t0, BLOCK)] = fade
        fall_ref[pl.ds(b * 8, 8)] = jnp.broadcast_to(grow[BLOCK - 1 : BLOCK], (8, INNER))
        xtb = (fade * act[pl.ds(t0, BLOCK), pl.ds(0, INNER)].astype(F32)).astype(BF16)
        gtb = (grow * cot_ref[pl.ds(t0, BLOCK)].astype(F32)).astype(BF16)
        xt[pl.ds(t0, BLOCK)] = xtb
        gt[pl.ds(t0, BLOCK)] = gtb
        bc = act[pl.ds(t0, BLOCK), pl.ds(INNER, 2 * STATE)]
        piece[pl.ds(b * STATE, STATE)] = mm(bc, xtb, 0, 0)[:STATE]
        back[pl.ds(b * STATE, STATE)] = mm(bc, gtb, 0, 0)[STATE:]

    state = jnp.zeros((STATE, INNER), F32)
    adj = jnp.zeros((STATE, INNER), F32)
    for b in range(blocks):
        state = fall_ref[pl.ds(b * 8, 1)] * (state + piece[pl.ds(b * STATE, STATE)])
    for b in reversed(range(blocks)):
        adj = fall_ref[pl.ds(b * 8, 1)] * adj + back[pl.ds(b * STATE, STATE)]
    top, low = pl.ds(0, SLICE), pl.ds(SLICE, SLICE)
    for j in range(MEMBERS):
        for c in range(CUTS):
            part = slice(c * WIDTH, (c + 1) * WIDTH)
            msg[j, c, top] = state[j * SLICE : (j + 1) * SLICE, part].astype(BF16)
            msg[j, c, low] = adj[j * SLICE : (j + 1) * SLICE, part].astype(BF16)

    def round1(off, c):
        to = (m + off) % MEMBERS
        return remote(msg.at[to, c], r1.at[m, c], s1.at[off, c], q1.at[off, c], base + to)

    def round1_in(off, c):
        frm = (m + MEMBERS - off) % MEMBERS
        return remote(msg.at[frm, c], r1.at[frm, c], s1.at[off, c], q1.at[off, c], base + frm)

    for c in range(CUTS):
        for off in range(1, MEMBERS):
            round1(off, c).start()
    r1[m] = msg[m]

    def intra(b):
        t0 = b * BLOCK
        bc = act[pl.ds(t0, BLOCK), pl.ds(INNER, 2 * STATE)]
        xtb, gtb = xt[pl.ds(t0, BLOCK)], gt[pl.ds(t0, BLOCK)]
        scores = mm(bc[:, STATE:], bc[:, :STATE], 1, 1)
        smb = jnp.where(causal, scores, 0.0).astype(BF16)
        u_ref[pl.ds(t0, BLOCK)] = mm(smb, xtb, 1, 0)
        v_ref[pl.ds(t0, BLOCK)] = mm(smb, gtb, 0, 0)
        ds_ref[pl.ds(t0, BLOCK)] = jnp.where(causal, mm(gtb, xtb, 1, 1), 0.0).astype(BF16)

    half = blocks // 2
    for b in range(half):
        intra(b)

    lax.fori_loop(1, n, decay_wait, 0)
    lines = [dall[base + i] for i in range(MEMBERS)]
    for q in range(groups):
        own = dall[q * MEMBERS]
        for i in range(1, MEMBERS):
            own = own * dall[q * MEMBERS + i]
        lines.append(own)
    spread128 = jnp.where((iota((128, INNER), 1) >> 5) == iota((128, INNER), 0), 1.0, 0.0)
    dexp[...] = mm(jnp.concatenate(lines, axis=0), spread128, 1, 0, EXACT)

    def round2(off, c):
        to = (g + off) % groups
        part = pl.ds(pl.multiple_of(jnp.where(to > g, 0, SLICE), SLICE), SLICE)
        return remote(
            msg2.at[c, part], r2.at[g, c, part], s2.at[off, c], q2.at[off, c], to * MEMBERS + m
        )

    def round2_in(off, c):
        frm = (g + groups - off) % groups
        part = pl.ds(pl.multiple_of(jnp.where(g > frm, 0, SLICE), SLICE), SLICE)
        return remote(
            msg2.at[c, part], r2.at[frm, c, part], s2.at[off, c], q2.at[off, c],
            frm * MEMBERS + m,
        )

    for c in range(CUTS):
        lanes = pl.ds(c * WIDTH, WIDTH)
        for off in range(1, MEMBERS):
            round1_in(off, c).wait_recv()
        gs = r1[0, c, top].astype(F32)
        for i in range(1, MEMBERS):
            gs = dexp[pl.ds(i * 8, 1), lanes] * gs + r1[i, c, top].astype(F32)
        ga = r1[MEMBERS - 1, c, low].astype(F32)
        for i in reversed(range(MEMBERS - 1)):
            ga = dexp[pl.ds(i * 8, 1), lanes] * ga + r1[i, c, low].astype(F32)
        msg2[c, top] = gs.astype(BF16)
        msg2[c, low] = ga.astype(BF16)
        for off in range(1, groups):
            round2(off, c).start()

    for b in range(half, blocks - 1):
        intra(b)

    def round3(off, c):
        to = (m + off) % MEMBERS
        return remote(msg3.at[to, c], r3.at[m, c], s3.at[off, c], q3.at[off, c], base + to)

    def round3_in(off, c):
        frm = (m + MEMBERS - off) % MEMBERS
        return remote(msg3.at[frm, c], r3.at[frm, c], s3.at[off, c], q3.at[off, c], base + frm)

    cin[...] = jnp.zeros((SLICE, INNER), F32)
    ain[...] = jnp.zeros((SLICE, INNER), F32)
    for c in range(CUTS):
        lanes = pl.ds(c * WIDTH, WIDTH)
        for off in range(1, groups):
            round2_in(off, c).wait_recv()
        for q in range(groups):
            @pl.when(q < g)
            def _(q=q):
                d = dexp[pl.ds((MEMBERS + q) * 8, 1), lanes]
                cin[:, lanes] = d * cin[:, lanes] + r2[q, c, top].astype(F32)
        for q in reversed(range(groups)):
            @pl.when(q > g)
            def _(q=q):
                d = dexp[pl.ds((MEMBERS + q) * 8, 1), lanes]
                ain[:, lanes] = d * ain[:, lanes] + r2[q, c, low].astype(F32)
        gs = cin[:, lanes]
        for i in range(MEMBERS):
            msg3[i, c, top] = gs.astype(BF16)
            gs = dexp[pl.ds(i * 8, 1), lanes] * gs + r1[i, c, top].astype(F32)
        ga = ain[:, lanes]
        for i in reversed(range(MEMBERS)):
            msg3[i, c, low] = ga.astype(BF16)
            ga = dexp[pl.ds(i * 8, 1), lanes] * ga + r1[i, c, low].astype(F32)
        for off in range(1, MEMBERS):
            round3(off, c).start()
    r3[m] = msg3[m]
    for b in range(blocks - 1, blocks):
        intra(b)
    skip = mm(jnp.broadcast_to(skip_ref[...], (8, HEADS)), spread_f, 1, 0, EXACT)[:1]
    skip_sum = jnp.zeros((1, INNER), F32)
    for b in range(blocks):
        rows_b = pl.ds(b * BLOCK, BLOCK)
        skip_sum = skip_sum + jnp.sum(
            cot_ref[rows_b].astype(F32) * act[rows_b, pl.ds(0, INNER)].astype(F32),
            axis=0, keepdims=True,
        )
    prm[...] = jnp.zeros((8, CONV), F32)
    prm[pl.ds(7, 1), pl.ds(0, HEADS)] = mm(
        jnp.broadcast_to(skip_sum, (8, INNER)), spread_f, 1, 1, EXACT
    )[:1]
    for c in range(CUTS):
        for off in range(1, MEMBERS):
            round3_in(off, c).wait_recv()

    def gathered(half_of):
        return jnp.concatenate(
            [
                jnp.concatenate([r3[i, c, half_of].astype(F32) for c in range(CUTS)], axis=1)
                for i in range(MEMBERS)
            ],
            axis=0,
        )

    state = gathered(top)
    adj = gathered(low)
    for b in range(blocks):
        part = pl.ds(b * STATE, STATE)
        fresh = fall_ref[pl.ds(b * 8, 1)] * (state + piece[part])
        piece[part] = state
        state = fresh
    tails = [None] * blocks
    for b in reversed(range(blocks)):
        part = pl.ds(b * STATE, STATE)
        after = state if b == blocks - 1 else piece[pl.ds((b + 1) * STATE, STATE)]
        tails[b] = jnp.sum(adj * after, axis=0, keepdims=True)
        lent = fall_ref[pl.ds(b * 8, 1)] * adj
        adj = lent + back[part]
        back[part] = lent

    def dz_copy():
        return remote(
            dz.at[pl.ds(0, 8)], dz_edge, dz_sem.at[0], dz_sem.at[1], jnp.maximum(me - 1, 0)
        )

    alog_sum = jnp.zeros((HEADS, BLOCK), F32)
    dtb_sum = jnp.zeros((HEADS, BLOCK), F32)
    last_row = iota((BLOCK, 1), 0) == BLOCK - 1
    for b in range(blocks):
        t0 = b * BLOCK
        here = pl.ds(t0, BLOCK)
        part = pl.ds(b * STATE, STATE)
        xtb, gtb = xt[here], gt[here]
        bc = act[here, pl.ds(INNER, 2 * STATE)]
        bm, cm = bc[:, :STATE], bc[:, STATE:]
        carry_b = piece[part].astype(BF16)
        lent_b = back[part].astype(BF16)
        u = u_ref[here] + mm(cm, carry_b, 1, 0)
        v = v_ref[here] + mm(bm, lent_b, 1, 0)
        taken = xtb.astype(F32) * v
        moved = gtb.astype(F32) * u - taken + jnp.where(last_row, tails[b], 0.0)
        gcum = per_head(moved)
        step_b = step_ref[:, here]
        grate = mm(gcum, tri, 1, 1, EXACT)
        gstep = per_head(taken) / step_b + neg_a * grate
        alog_sum = alog_sum + grate * (neg_a * step_b)
        graw = gstep * sig_ref[:, here]
        gdt_ref[:, here] = graw
        dtb_sum = dtb_sum + graw
        gact = fx[here] * v + skip * cot_ref[here].astype(F32)
        dz[here, pl.ds(0, INNER)] = gact * dsil[here, pl.ds(0, INNER)]
        ds = ds_ref[here]
        gb = mm(ds, cm, 0, 0) + mm(xtb, lent_b, 1, 1)
        gc = mm(ds, bm, 1, 0) + mm(gtb, carry_b, 1, 1)
        dz[here, pl.ds(INNER, 2 * STATE)] = (
            jnp.concatenate([gb, gc], axis=1) * dsil[here, pl.ds(INNER, 2 * STATE)]
        )
        if b == 0:
            @pl.when(me > 0)
            def _():
                dz_copy().start()

    ones = jnp.ones((8, BLOCK), F32)
    prm[pl.ds(5, 1), pl.ds(0, HEADS)] = mm(ones, dtb_sum, 1, 1, EXACT)[:1]
    prm[pl.ds(6, 1), pl.ds(0, HEADS)] = mm(ones, alog_sum, 1, 1, EXACT)[:1]
    for j in range(CONV // 128):
        lanes = pl.ds(j * 128, 128)
        total = [jnp.zeros((8, 128), F32) for _ in range(5)]
        for b in range(blocks):
            t0 = b * BLOCK
            grad = dz[pl.ds(t0, BLOCK), lanes]
            for k in range(4):
                total[k] = total[k] + jnp.sum(
                    (grad * xs[pl.ds(t0 + 5 + k, BLOCK), lanes]).reshape(BLOCK // 8, 8, 128), axis=0
                )
            total[4] = total[4] + jnp.sum(grad.reshape(BLOCK // 8, 8, 128), axis=0)
        for k in range(5):
            prm[pl.ds(k, 1), lanes] = jnp.sum(total[k], axis=0, keepdims=True)

    def sum1(off):
        to = (m + off) % MEMBERS
        return remote(prm, p1.at[m], s4.at[off], q4.at[off], base + to)

    def sum1_in(off):
        frm = (m + MEMBERS - off) % MEMBERS
        return remote(prm, p1.at[frm], s4.at[off], q4.at[off], base + frm)

    def sum2(off):
        to = (g + off) % groups
        return remote(p2s, p2.at[g], s5.at[off], q5.at[off], to * MEMBERS + m)

    def sum2_in(off):
        frm = (g + groups - off) % groups
        return remote(p2s, p2.at[frm], s5.at[off], q5.at[off], frm * MEMBERS + m)

    for off in range(1, MEMBERS):
        sum1(off).start()
    p1[m] = prm[...]

    def data_grad(b):
        t0 = b * BLOCK
        for j in range(CONV // 128):
            lanes = pl.ds(j * 128, 128)
            total = w_ref[pl.ds(0, 1), lanes] * dz[pl.ds(t0 + 3, BLOCK), lanes]
            for k in range(1, 4):
                total = total + w_ref[pl.ds(k, 1), lanes] * dz[pl.ds(t0 + 3 - k, BLOCK), lanes]
            gx_ref[pl.ds(t0, BLOCK), lanes] = total.astype(BF16)

    for b in range(half):
        data_grad(b)
    for off in range(1, MEMBERS):
        sum1_in(off).wait_recv()
    p2s[...] = (p1[0] + p1[1]) + (p1[2] + p1[3])
    for off in range(1, groups):
        sum2(off).start()
    p2[g] = p2s[...]
    dz[pl.ds(rows, 8)] = jnp.zeros((8, CONV), F32)

    @pl.when(me < n - 1)
    def _():
        dz_copy().wait_recv()
        dz[pl.ds(rows, 8)] = dz_edge[...]

    for b in range(half, blocks):
        data_grad(b)
    for off in range(1, groups):
        sum2_in(off).wait_recv()
    total = p2[0]
    for q in range(1, groups):
        total = total + p2[q]
    sums_ref[...] = total

    @pl.when(me < n - 1)
    def _():
        edge_copy().wait_send()

    @pl.when(me > 0)
    def _():
        dz_copy().wait_send()

    for off in range(1, MEMBERS):
        for c in range(CUTS):
            round1(off, c).wait_send()
            round3(off, c).wait_send()
        sum1(off).wait_send()
    for off in range(1, groups):
        for c in range(CUTS):
            round2(off, c).wait_send()
        sum2(off).wait_send()
    lax.fori_loop(1, n, decay_sent, 0)


def finish(gx_in, gdt_in, sums, gx_ref, gdt_ref, gw_ref, gbias_ref, gdtb_ref, galog_ref, gskip_ref):
    gx_ref[...] = gx_in[...]
    gdt_ref[...] = gdt_in[...]
    gw_ref[...] = sums[pl.ds(0, 4)]
    gbias_ref[...] = sums[pl.ds(4, 1)].reshape(CONV)
    gdtb_ref[...] = sums[pl.ds(5, 1), pl.ds(0, HEADS)].reshape(HEADS)
    galog_ref[...] = sums[pl.ds(6, 1), pl.ds(0, HEADS)].reshape(HEADS)
    gskip_ref[...] = sums[pl.ds(7, 1), pl.ds(0, HEADS)].reshape(HEADS)


def local(n, xbc, dt_raw, cotangent, conv_weight, conv_bias, dt_bias, a_log, d_skip):
    rows = xbc.shape[0]
    blocks = rows // BLOCK
    groups = n // MEMBERS
    vmem = pl.BlockSpec(memory_space=pltpu.VMEM)
    dma = pltpu.SemaphoreType.DMA
    outs = pl.pallas_call(
        functools.partial(kernel, n),
        out_shape=(
            jax.ShapeDtypeStruct((rows, CONV), BF16),
            jax.ShapeDtypeStruct((HEADS, rows), F32),
            jax.ShapeDtypeStruct((8, CONV), F32),
        ),
        in_specs=[vmem] * 8,
        out_specs=(vmem,) * 3,
        scratch_shapes=[
            pltpu.VMEM((rows + 8, CONV), F32),
            pltpu.VMEM((16, CONV), BF16),
            pltpu.VMEM((rows, CONV), BF16),
            pltpu.VMEM((rows, CONV), F32),
            pltpu.VMEM((rows, INNER), BF16),
            pltpu.VMEM((rows, INNER), BF16),
            pltpu.VMEM((rows, INNER), F32),
            pltpu.VMEM((rows, INNER), F32),
            pltpu.VMEM((rows, INNER), F32),
            pltpu.VMEM((rows, BLOCK), BF16),
            pltpu.VMEM((blocks * STATE, INNER), F32),
            pltpu.VMEM((blocks * STATE, INNER), F32),
            pltpu.VMEM((blocks * 8, INNER), F32),
            pltpu.VMEM((HEADS, rows), F32),
            pltpu.VMEM((HEADS, rows), F32),
            pltpu.VMEM((MEMBERS, CUTS, 2 * SLICE, WIDTH), BF16),
            pltpu.VMEM((MEMBERS, CUTS, 2 * SLICE, WIDTH), BF16),
            pltpu.VMEM((CUTS, 2 * SLICE, WIDTH), BF16),
            pltpu.VMEM((groups, CUTS, 2 * SLICE, WIDTH), BF16),
            pltpu.VMEM((MEMBERS, CUTS, 2 * SLICE, WIDTH), BF16),
            pltpu.VMEM((MEMBERS, CUTS, 2 * SLICE, WIDTH), BF16),
            pltpu.VMEM((SLICE, INNER), F32),
            pltpu.VMEM((SLICE, INNER), F32),
            pltpu.VMEM((rows + 8, CONV), F32),
            pltpu.VMEM((8, CONV), F32),
            pltpu.VMEM((8, CONV), F32),
            pltpu.VMEM((MEMBERS, 8, CONV), F32),
            pltpu.VMEM((8, CONV), F32),
            pltpu.VMEM((groups, 8, CONV), F32),
            pltpu.VMEM((8, 128), F32),
            pltpu.VMEM((n, 8, 128), F32),
            pltpu.VMEM(((MEMBERS + groups) * 8, INNER), F32),
            dma((2,)),
            dma((MEMBERS, CUTS)), dma((MEMBERS, CUTS)),
            dma((groups, CUTS)), dma((groups, CUTS)),
            dma((MEMBERS, CUTS)), dma((MEMBERS, CUTS)),
            dma((2,)),
            dma((MEMBERS,)), dma((MEMBERS,)),
            dma((groups,)), dma((groups,)),
            dma((n,)), dma((n,)),
        ],
        compiler_params=pltpu.CompilerParams(
            collective_id=0, has_side_effects=True, vmem_limit_bytes=56 * 1024 * 1024
        ),
        cost_estimate=pl.CostEstimate(
            flops=2 * 10**9, bytes_accessed=5 * 10**6, transcendentals=10**6
        ),
        name="mixer",
    )(
        xbc, dt_raw, cotangent, conv_weight, conv_bias,
        dt_bias.reshape(1, HEADS), a_log.reshape(1, HEADS), d_skip.reshape(1, HEADS),
    )
    return pl.pallas_call(
        finish,
        out_shape=(
            jax.ShapeDtypeStruct((rows, CONV), BF16),
            jax.ShapeDtypeStruct((HEADS, rows), F32),
            jax.ShapeDtypeStruct((4, CONV), F32),
            jax.ShapeDtypeStruct((CONV,), F32),
            jax.ShapeDtypeStruct((HEADS,), F32),
            jax.ShapeDtypeStruct((HEADS,), F32),
            jax.ShapeDtypeStruct((HEADS,), F32),
        ),
        in_specs=[vmem] * 3,
        out_specs=(vmem,) * 7,
        compiler_params=pltpu.CompilerParams(vmem_limit_bytes=56 * 1024 * 1024),
        name="finish",
    )(*outs)


def solution(mesh):
    sequence = P(("groups", "seq"), None)
    return jax.shard_map(
        functools.partial(local, mesh.shape["seq"]),
        mesh=mesh,
        in_specs=(sequence, P(None, ("groups", "seq")), sequence, P(), P(), P(), P(), P()),
        out_specs=(
            sequence, P(None, ("groups", "seq")), P("groups", None),
            P("groups"), P("groups"), P("groups"), P("groups"),
        ),
        check_vma=False,
    )
```
